32 devices in a mesh: grp: 4 (over z), dev: 8 (over y, x, core).
Axes of the slice: x: 2, y: 2, z: 4, core: 2. Of those that a mesh axis runs over, the one named last changes fastest.
Arguments:
- amplitudes: bfloat16 [1024, 589824], P('dev', 'grp'), may hold values from -6 to 6
- singles: float32 [32, 768], replicated, may hold values from -5 to 5
- pair_source: int32 [1024], replicated, may hold values from 0 to 1023, each once
- integrals: bfloat16 [589824, 512], P(('grp', 'dev')), may hold values from -0.0078125 to 0.0078125
Outputs:
- ladder: float32 [1024, 512], P('dev')
The draws below stay inside these ranges and needn't reach their ends.
Inputs may be any that keep to these rules, and one draw needn't show every extreme that they name: `pair_source`: each occupied pair appears exactly once.
All inputs are finite; a program needn't handle non-finite values.
Results may differ from the reference program's by a relative error of at most 0.0029.
Values may be sent and summed in bfloat16 or wider, within the bound.
A program may use at most 320 MiB of HBM per device.

```python
import jax
import jax.numpy as jnp
from jax import lax

O = 32
V = 768
AB = 512
IJ = 1024
CD = 589824


def levels(key, extent, cuts, smallest, largest):
    level = 1.0
    for axis_at, shards_of in cuts:
        steps = jax.random.uniform(jax.random.fold_in(jax.random.fold_in(key, 6), axis_at), (shards_of,), jnp.float32, smallest / len(cuts), largest / len(cuts))
        level = level * jnp.repeat(jnp.exp(steps), extent[axis_at] // shards_of).reshape((-1,) + (1,) * (len(extent) - 1 - axis_at))
    return level


def bell_draw(stream_key, extent, spread, reach, cuts=(), kind=jnp.bfloat16):
    result = spread * jax.random.normal(stream_key, extent, jnp.float32)
    if cuts:
        result = result * levels(stream_key, extent, cuts, -0.22, 0.18)
    return jnp.clip(result, -reach, reach).astype(kind)


def setup_inputs(seed: int = 0) -> dict:
    keys = jax.random.split(jax.random.key(seed), 5)
    amplitudes = bell_draw(keys[0], (IJ, CD), 1.0, 6.0, ((0, 8), (1, 4)))
    singles = bell_draw(keys[1], (O, V), 0.7, 5.0, (), jnp.float32)
    pair_source = jax.random.permutation(keys[2], O * O).astype(jnp.int32)
    integrals = bell_draw(keys[3], (CD, AB), (V * V) ** -0.5, 0.0078125, ((0, 32),))
    return dict(amplitudes=amplitudes, singles=singles, pair_source=pair_source, integrals=integrals)


def reference(amplitudes, singles, pair_source, integrals):
    def one_block(total, c_index):
        start = (c_index * V).astype(jnp.int32)
        block = lax.dynamic_slice_in_dim(amplitudes, start, V, 1)
        block = jnp.take(block, pair_source, axis=0)
        column = lax.dynamic_slice_in_dim(singles, c_index.astype(jnp.int32), 1, 1)[:, 0]
        dressing = (column[:, None, None] * singles[None, :, :]).reshape(O * O, V)
        tau = (block.astype(jnp.float32) + dressing).astype(jnp.bfloat16)
        rows = lax.dynamic_slice_in_dim(integrals, start, V, 0)
        return total + jnp.dot(tau, rows, preferred_element_type=jnp.float32), None

    total = jnp.zeros((O * O, AB), jnp.float32)
    total, unused = lax.scan(one_block, total, jnp.arange(V, dtype=jnp.int32))
    return total
```

```python
import functools

import jax
import jax.numpy as jnp
from jax import lax
from jax.experimental import pallas as pl
from jax.experimental.pallas import tpu as pltpu
from jax.sharding import PartitionSpec as P

MESH = pl.DeviceIdType.MESH
CHUNK = 16
WINDOW = 2


def kernel(n, occupied, virtual, amp, integrals, pair, column, out, dress, recv,
           held, tile, total, send_sem, recv_sem, load_sem, held_sem):
    me = lax.axis_index("dev")
    rows = out.shape[1]
    count = integrals.shape[0]
    width = integrals.shape[1]
    chunks = rows // CHUNK
    blocks = count // virtual
    window = min(WINDOW, chunks)

    load_integrals = pltpu.make_async_copy(integrals, held, held_sem)
    load_integrals.start()

    barrier = pltpu.get_barrier_semaphore()
    for o in range(1, n):
        pl.semaphore_signal(barrier, inc=1, device_id={"dev": lax.rem(me + o, n)}, device_id_type=MESH)
    pl.semaphore_wait(barrier, n - 1)

    def span(q):
        return pl.ds(pl.multiple_of(q * CHUNK, CHUNK), CHUNK)

    def remote(o, q):
        peer = lax.rem(me + o, n)
        return pltpu.make_async_remote_copy(
            src_ref=amp.at[span(q), pl.ds(pl.multiple_of(peer * count, 128), count)],
            dst_ref=recv.at[o - 1, span(q), :],
            send_sem=send_sem.at[o - 1, q],
            recv_sem=recv_sem.at[o - 1, q],
            device_id={"dev": peer},
            device_id_type=MESH,
        )

    def load(o, q):
        if o == 0:
            source = amp.at[span(q), pl.ds(pl.multiple_of(me * count, 128), count)]
        else:
            source = recv.at[o - 1, span(q), :]
        return pltpu.make_async_copy(source, tile.at[lax.rem(me - o + n, n)], load_sem.at[o])

    order = list(range(n - 1, 0, -1))
    for q in range(window):
        for o in order:
            remote(o, q).start()

    dress[...] = jnp.zeros_like(dress)
    load_integrals.wait()

    def dress_one(c, carry):
        both = jnp.dot(pair[...], held[pl.ds(pl.multiple_of(c * virtual, virtual), virtual), :],
                       preferred_element_type=jnp.float32)
        inner = both[:occupied] + both[occupied:]

        def one_row(i, carry):
            dress[i] += column[c, i] * inner
            return carry

        return lax.fori_loop(0, occupied, one_row, carry)

    lax.fori_loop(0, blocks, dress_one, 0)

    def chunk(q, carry):
        for o in order:
            remote(o, q).wait_send()

        @pl.when(q + window < chunks)
        def _():
            for o in order:
                remote(o, q + window).start()

        for o in order:
            remote(o, q).wait_recv()
        for o in range(n):
            load(o, q).start()
        for o in range(n):
            load(o, q).wait()
        total[...] = jnp.zeros_like(total)

        def term(k, carry):
            part = pl.ds(pl.multiple_of(k * virtual, virtual), virtual)
            total[...] += jnp.dot(tile[:, :, part].reshape(n * CHUNK, virtual), held[part, :],
                                  preferred_element_type=jnp.float32)
            return carry

        lax.fori_loop(0, blocks, term, 0)
        out[:, span(q), :] = total[...].reshape(n, CHUNK, width)
        return carry

    lax.fori_loop(0, chunks, chunk, 0)


def split_pair(singles):
    high = lax.reduce_precision(singles, 8, 7)
    low = lax.reduce_precision(singles - high, 8, 7)
    return jnp.concatenate([high, low], 0).astype(jnp.bfloat16)


def body(amplitudes, singles, pair_source, integrals):
    n = lax.axis_size("dev")
    occupied, virtual = singles.shape
    rows = amplitudes.shape[0]
    count, width = integrals.shape
    chunks = rows // CHUNK
    blocks = count // virtual
    first = (lax.axis_index("grp") * n + lax.axis_index("dev")) * blocks
    column = lax.dynamic_slice_in_dim(singles.T, first, blocks, 0)
    any_spec = pl.BlockSpec(memory_space=pl.ANY)
    vmem = pl.BlockSpec(memory_space=pltpu.VMEM)
    smem = pl.BlockSpec(memory_space=pltpu.SMEM)
    partial, dress, _ = pl.pallas_call(
        functools.partial(kernel, n, occupied, virtual),
        out_shape=(
            jax.ShapeDtypeStruct((n, rows, width), jnp.float32),
            jax.ShapeDtypeStruct((occupied, occupied, width), jnp.float32),
            jax.ShapeDtypeStruct((n - 1, rows, count), jnp.bfloat16),
        ),
        in_specs=[any_spec, any_spec, vmem, smem],
        out_specs=(vmem, vmem, any_spec),
        scratch_shapes=[
            pltpu.VMEM((count, width), jnp.bfloat16),
            pltpu.VMEM((n, CHUNK, count), jnp.bfloat16),
            pltpu.VMEM((n * CHUNK, width), jnp.float32),
            pltpu.SemaphoreType.DMA((n - 1, chunks)),
            pltpu.SemaphoreType.DMA((n - 1, chunks)),
            pltpu.SemaphoreType.DMA((n,)),
            pltpu.SemaphoreType.DMA,
        ],
        compiler_params=pltpu.CompilerParams(
            collective_id=0, has_side_effects=True, vmem_limit_bytes=48 * 1024 * 1024
        ),
        cost_estimate=pl.CostEstimate(
            flops=2 * n * rows * count * width,
            bytes_accessed=4 * n * rows * count + 2 * count * width,
            transcendentals=0,
        ),
    )(amplitudes, integrals, split_pair(singles), column)
    whole = jnp.take(partial.reshape(n * rows, width), pair_source, axis=0)
    whole = whole + dress.reshape(n * rows, width)
    mine = lax.psum_scatter(whole, "dev", scatter_dimension=0, tiled=True)
    return lax.psum(mine, "grp")


def solution(mesh):
    placed = (P("dev", "grp"), P(), P(), P(("grp", "dev"), None))
    return jax.shard_map(
        body, mesh=mesh, in_specs=placed, out_specs=P("dev", None), check_vma=False
    )
```

```python
import functools

import jax
import jax.numpy as jnp
from jax import lax
from jax.experimental import pallas as pl
from jax.experimental.pallas import tpu as pltpu
from jax.sharding import PartitionSpec as P

MESH = pl.DeviceIdType.MESH
CHUNK = 16
WINDOW = 2


def kernel(n, occupied, virtual, amp, integrals, pair, column, out, dress, recv,
           held, tile, total, send_sem, recv_sem, load_sem, held_sem):
    me = lax.axis_index("dev")
    rows = out.shape[1]
    count = integrals.shape[0]
    width = integrals.shape[1]
    chunks = rows // CHUNK
    blocks = count // virtual
    window = min(WINDOW, chunks)

    load_integrals = pltpu.make_async_copy(integrals, held, held_sem)
    load_integrals.start()

    barrier = pltpu.get_barrier_semaphore()
    for o in range(1, n):
        pl.semaphore_signal(barrier, inc=1, device_id={"dev": lax.rem(me + o, n)}, device_id_type=MESH)
    pl.semaphore_wait(barrier, n - 1)

    def span(q):
        return pl.ds(pl.multiple_of(q * CHUNK, CHUNK), CHUNK)

    def remote(o, q):
        peer = lax.rem(me + o, n)
        return pltpu.make_async_remote_copy(
            src_ref=amp.at[span(q), pl.ds(pl.multiple_of(peer * count, 128), count)],
            dst_ref=recv.at[o - 1, span(q), :],
            send_sem=send_sem.at[o - 1, q],
            recv_sem=recv_sem.at[o - 1, q],
            device_id={"dev": peer},
            device_id_type=MESH,
        )

    def load(o, q):
        if o == 0:
            source = amp.at[span(q), pl.ds(pl.multiple_of(me * count, 128), count)]
        else:
            source = recv.at[o - 1, span(q), :]
        return pltpu.make_async_copy(source, tile.at[lax.rem(me - o + n, n)], load_sem.at[o])

    order = list(range(n - 1, 0, -1))
    for q in range(window):
        for o in order:
            remote(o, q).start()

    dress[...] = jnp.zeros_like(dress)
    load_integrals.wait()

    def dress_one(c, carry):
        both = jnp.dot(pair[...], held[pl.ds(pl.multiple_of(c * virtual, virtual), virtual), :],
                       preferred_element_type=jnp.float32)
        inner = both[:occupied] + both[occupied:]

        def one_row(i, carry):
            dress[i] += column[c, i] * inner
            return carry

        return lax.fori_loop(0, occupied, one_row, carry)

    lax.fori_loop(0, blocks, dress_one, 0)

    def chunk(q, carry):
        for o in order:
            remote(o, q).wait_send()

        @pl.when(q + window < chunks)
        def _():
            for o in order:
                remote(o, q + window).start()

        for o in order:
            remote(o, q).wait_recv()
        for o in range(n):
            load(o, q).start()
        for o in range(n):
            load(o, q).wait()
        total[...] = jnp.zeros_like(total)

        def term(k, carry):
            part = pl.ds(pl.multiple_of(k * virtual, virtual), virtual)
            total[...] += jnp.dot(tile[:, :, part].reshape(n * CHUNK, virtual), held[part, :],
                                  preferred_element_type=jnp.float32)
            return carry

        lax.fori_loop(0, blocks, term, 0)
        out[:, span(q), :] = total[...].reshape(n, CHUNK, width)
        return carry

    lax.fori_loop(0, chunks, chunk, 0)


def split_pair(singles):
    high = lax.reduce_precision(singles, 8, 7)
    low = lax.reduce_precision(singles - high, 8, 7)
    return jnp.concatenate([high, low], 0).astype(jnp.bfloat16)


def body(amplitudes, singles, pair_source, integrals):
    n = lax.axis_size("dev")
    occupied, virtual = singles.shape
    rows = amplitudes.shape[0]
    count, width = integrals.shape
    chunks = rows // CHUNK
    blocks = count // virtual
    first = (lax.axis_index("grp") * n + lax.axis_index("dev")) * blocks
    column = lax.dynamic_slice_in_dim(singles.T, first, blocks, 0)
    any_spec = pl.BlockSpec(memory_space=pl.ANY)
    vmem = pl.BlockSpec(memory_space=pltpu.VMEM)
    smem = pl.BlockSpec(memory_space=pltpu.SMEM)
    partial, dress, _ = pl.pallas_call(
        functools.partial(kernel, n, occupied, virtual),
        out_shape=(
            jax.ShapeDtypeStruct((n, rows, width), jnp.float32),
            jax.ShapeDtypeStruct((occupied, occupied, width), jnp.float32),
            jax.ShapeDtypeStruct((n - 1, rows, count), jnp.bfloat16),
        ),
        in_specs=[any_spec, any_spec, vmem, smem],
        out_specs=(vmem, vmem, any_spec),
        scratch_shapes=[
            pltpu.VMEM((count, width), jnp.bfloat16),
            pltpu.VMEM((n, CHUNK, count), jnp.bfloat16),
            pltpu.VMEM((n * CHUNK, width), jnp.float32),
            pltpu.SemaphoreType.DMA((n - 1, chunks)),
            pltpu.SemaphoreType.DMA((n - 1, chunks)),
            pltpu.SemaphoreType.DMA((n,)),
            pltpu.SemaphoreType.DMA,
        ],
        compiler_params=pltpu.CompilerParams(
            collective_id=0, has_side_effects=True, vmem_limit_bytes=48 * 1024 * 1024
        ),
        cost_estimate=pl.CostEstimate(
            flops=2 * n * rows * count * width,
            bytes_accessed=4 * n * rows * count + 2 * count * width,
            transcendentals=0,
        ),
    )(amplitudes, integrals, split_pair(singles), column)
    whole = jnp.take(partial.reshape(n * rows, width), pair_source, axis=0)
    whole = whole + dress.reshape(n * rows, width)
    whole = whole.reshape(n, n * rows // n, width)
    mine = lax.all_to_all(whole, "dev", split_axis=0, concat_axis=0, tiled=True).sum(0)
    return lax.all_gather(mine, "grp").sum(0)


def solution(mesh):
    placed = (P("dev", "grp"), P(), P(), P(("grp", "dev"), None))
    return jax.shard_map(
        body, mesh=mesh, in_specs=placed, out_specs=P("dev", None), check_vma=False
    )
```

```python
import functools

import jax
import jax.numpy as jnp
from jax import lax
from jax.experimental import pallas as pl
from jax.experimental.pallas import tpu as pltpu
from jax.sharding import PartitionSpec as P

MESH = pl.DeviceIdType.MESH
CHUNK = 16
WINDOW = 2


def kernel(n, occupied, virtual, amp, integrals, pair, column, out, dress, recv,
           held, tile, total, send_sem, recv_sem, load_sem, held_sem):
    me = lax.axis_index("dev")
    rows = out.shape[1]
    count = integrals.shape[0]
    width = integrals.shape[1]
    chunks = rows // CHUNK
    blocks = count // virtual
    window = min(WINDOW, chunks)

    load_integrals = pltpu.make_async_copy(integrals, held, held_sem)
    load_integrals.start()

    barrier = pltpu.get_barrier_semaphore()
    for o in range(1, n):
        pl.semaphore_signal(barrier, inc=1, device_id={"dev": lax.rem(me + o, n)}, device_id_type=MESH)
    pl.semaphore_wait(barrier, n - 1)

    def span(q):
        return pl.ds(pl.multiple_of(q * CHUNK, CHUNK), CHUNK)

    def remote(o, q):
        peer = lax.rem(me + o, n)
        return pltpu.make_async_remote_copy(
            src_ref=amp.at[span(q), pl.ds(pl.multiple_of(peer * count, 128), count)],
            dst_ref=recv.at[o - 1, span(q), :],
            send_sem=send_sem.at[o - 1, q],
            recv_sem=recv_sem.at[o - 1, q],
            device_id={"dev": peer},
            device_id_type=MESH,
        )

    def load(o, q):
        if o == 0:
            source = amp.at[span(q), pl.ds(pl.multiple_of(me * count, 128), count)]
        else:
            source = recv.at[o - 1, span(q), :]
        return pltpu.make_async_copy(source, tile.at[lax.rem(me - o + n, n)], load_sem.at[o])

    order = list(range(n - 1, 0, -1))
    for q in range(window):
        for o in order:
            remote(o, q).start()

    dress[...] = jnp.zeros_like(dress)
    load_integrals.wait()

    def dress_one(c, carry):
        both = jnp.dot(pair[...], held[pl.ds(pl.multiple_of(c * virtual, virtual), virtual), :],
                       preferred_element_type=jnp.float32)
        inner = both[:occupied] + both[occupied:]

        def one_row(i, carry):
            dress[i] += column[c, i] * inner
            return carry

        return lax.fori_loop(0, occupied, one_row, carry)

    lax.fori_loop(0, blocks, dress_one, 0)

    def chunk(q, carry):
        for o in order:
            remote(o, q).wait_send()

        @pl.when(q + window < chunks)
        def _():
            for o in order:
                remote(o, q + window).start()

        for o in order:
            remote(o, q).wait_recv()
        for o in range(n):
            load(o, q).start()
        for o in range(n):
            load(o, q).wait()
        total[...] = jnp.zeros_like(total)

        def term(k, carry):
            part = pl.ds(pl.multiple_of(k * virtual, virtual), virtual)
            total[...] += jnp.dot(tile[:, :, part].reshape(n * CHUNK, virtual), held[part, :],
                                  preferred_element_type=jnp.float32)
            return carry

        lax.fori_loop(0, blocks, term, 0)
        out[:, span(q), :] = total[...].reshape(n, CHUNK, width)
        return carry

    lax.fori_loop(0, chunks, chunk, 0)


def combine(n, g, whole, out, half, summed, got, mine, zgot, full,
            half_send, half_recv, got_send, got_recv, z_send, z_recv, full_send, full_recv):
    me = lax.axis_index("dev")
    z = lax.axis_index("grp")
    m = n // 2
    side = lax.rem(me, 2)
    base = me // 2
    mate = me + 1 - 2 * side
    piece = out.shape[0] // g

    def peer(o):
        return 2 * lax.rem(base + o, m) + side

    def zpeer(o):
        return lax.rem(z + o, g)

    barrier = pltpu.get_barrier_semaphore()
    for target in [mate] + [peer(o) for o in range(1, m)]:
        pl.semaphore_signal(barrier, inc=1, device_id={"dev": target}, device_id_type=MESH)
    for o in range(1, g):
        pl.semaphore_signal(barrier, inc=1, device_id={"grp": zpeer(o)}, device_id_type=MESH)
    pl.semaphore_wait(barrier, 1 + (m - 1) + (g - 1))

    def slab(i):
        return pl.ds(pl.multiple_of(i * piece, piece), piece)

    def to_mate(o):
        return pltpu.make_async_remote_copy(
            src_ref=whole.at[lax.rem(base + o, m), 1 - side], dst_ref=half.at[o],
            send_sem=half_send.at[o], recv_sem=half_recv.at[o],
            device_id={"dev": mate}, device_id_type=MESH)

    def to_peer(o):
        return pltpu.make_async_remote_copy(
            src_ref=summed.at[o], dst_ref=got.at[o - 1],
            send_sem=got_send.at[o - 1], recv_sem=got_recv.at[o - 1],
            device_id={"dev": peer(o)}, device_id_type=MESH)

    def to_owner(o):
        return pltpu.make_async_remote_copy(
            src_ref=mine.at[slab(zpeer(o)), :], dst_ref=zgot.at[o - 1],
            send_sem=z_send.at[o - 1], recv_sem=z_recv.at[o - 1],
            device_id={"grp": zpeer(o)}, device_id_type=MESH)

    def to_all(o, slot):
        return pltpu.make_async_remote_copy(
            src_ref=full.at[slab(slot), :], dst_ref=full.at[slab(slot), :],
            send_sem=full_send.at[o - 1], recv_sem=full_recv.at[o - 1],
            device_id={"grp": zpeer(o)}, device_id_type=MESH)

    order = list(range(1, m)) + [0]
    for o in order:
        to_mate(o).start()
    for o in order:
        to_mate(o).wait_recv()
        summed[o] = whole[lax.rem(base + o, m), side] + half[o]
        if o:
            to_peer(o).start()
    value = summed[0]
    for o in range(1, m):
        to_peer(o).wait_recv()
        value = value + got[o - 1]
    mine[...] = value
    for o in range(1, g):
        to_owner(o).start()
    part = mine[slab(z), :]
    for o in range(1, g):
        to_owner(o).wait_recv()
        part = part + zgot[o - 1]
    full[slab(z), :] = part
    for o in range(1, g):
        to_all(o, z).start()
    for o in range(1, g):
        to_all(o, lax.rem(z - o + g, g)).wait_recv()
    for o in order:
        to_mate(o).wait_send()
    for o in range(1, m):
        to_peer(o).wait_send()
    for o in range(1, g):
        to_owner(o).wait_send()
        to_all(o, z).wait_send()
    out[...] = full[...]


def reduce_devices(whole):
    n, g = lax.axis_size("dev"), lax.axis_size("grp")
    share, width = whole.shape[0] // n, whole.shape[1]
    if n % 2 or n < 4 or g < 2 or share % (8 * g):
        whole = whole.reshape(n, share, width)
        mine = lax.all_to_all(whole, "dev", split_axis=0, concat_axis=0, tiled=True).sum(0)
        return lax.all_gather(mine, "grp").sum(0)
    m = n // 2
    vmem = pl.BlockSpec(memory_space=pltpu.VMEM)
    f32 = jnp.float32
    dma = pltpu.SemaphoreType.DMA
    return pl.pallas_call(
        functools.partial(combine, n, g),
        out_shape=jax.ShapeDtypeStruct((share, width), f32),
        in_specs=[vmem],
        out_specs=vmem,
        scratch_shapes=[
            pltpu.VMEM((m, share, width), f32),
            pltpu.VMEM((m, share, width), f32),
            pltpu.VMEM((m - 1, share, width), f32),
            pltpu.VMEM((share, width), f32),
            pltpu.VMEM((g - 1, share // g, width), f32),
            pltpu.VMEM((share, width), f32),
            dma((m,)), dma((m,)), dma((m - 1,)), dma((m - 1,)),
            dma((g - 1,)), dma((g - 1,)), dma((g - 1,)), dma((g - 1,)),
        ],
        compiler_params=pltpu.CompilerParams(
            collective_id=1, has_side_effects=True, vmem_limit_bytes=32 * 1024 * 1024
        ),
    )(whole.reshape(m, 2, share, width))


def split_pair(singles):
    high = lax.reduce_precision(singles, 8, 7)
    low = lax.reduce_precision(singles - high, 8, 7)
    return jnp.concatenate([high, low], 0).astype(jnp.bfloat16)


def body(amplitudes, singles, pair_source, integrals):
    n = lax.axis_size("dev")
    occupied, virtual = singles.shape
    rows = amplitudes.shape[0]
    count, width = integrals.shape
    chunks = rows // CHUNK
    blocks = count // virtual
    first = (lax.axis_index("grp") * n + lax.axis_index("dev")) * blocks
    column = lax.dynamic_slice_in_dim(singles.T, first, blocks, 0)
    any_spec = pl.BlockSpec(memory_space=pl.ANY)
    vmem = pl.BlockSpec(memory_space=pltpu.VMEM)
    smem = pl.BlockSpec(memory_space=pltpu.SMEM)
    partial, dress, _ = pl.pallas_call(
        functools.partial(kernel, n, occupied, virtual),
        out_shape=(
            jax.ShapeDtypeStruct((n, rows, width), jnp.float32),
            jax.ShapeDtypeStruct((occupied, occupied, width), jnp.float32),
            jax.ShapeDtypeStruct((n - 1, rows, count), jnp.bfloat16),
        ),
        in_specs=[any_spec, any_spec, vmem, smem],
        out_specs=(vmem, vmem, any_spec),
        scratch_shapes=[
            pltpu.VMEM((count, width), jnp.bfloat16),
            pltpu.VMEM((n, CHUNK, count), jnp.bfloat16),
            pltpu.VMEM((n * CHUNK, width), jnp.float32),
            pltpu.SemaphoreType.DMA((n - 1, chunks)),
            pltpu.SemaphoreType.DMA((n - 1, chunks)),
            pltpu.SemaphoreType.DMA((n,)),
            pltpu.SemaphoreType.DMA,
        ],
        compiler_params=pltpu.CompilerParams(
            collective_id=0, has_side_effects=True, vmem_limit_bytes=48 * 1024 * 1024
        ),
        cost_estimate=pl.CostEstimate(
            flops=2 * n * rows * count * width,
            bytes_accessed=4 * n * rows * count + 2 * count * width,
            transcendentals=0,
        ),
    )(amplitudes, integrals, split_pair(singles), column)
    whole = jnp.take(partial.reshape(n * rows, width), pair_source, axis=0)
    whole = whole + dress.reshape(n * rows, width)
    return reduce_devices(whole)


def solution(mesh):
    placed = (P("dev", "grp"), P(), P(), P(("grp", "dev"), None))
    return jax.shard_map(
        body, mesh=mesh, in_specs=placed, out_specs=P("dev", None), check_vma=False
    )
```

```python
import functools

import jax
import jax.numpy as jnp
from jax import lax
from jax.experimental import pallas as pl
from jax.experimental.pallas import tpu as pltpu
from jax.sharding import PartitionSpec as P

MESH = pl.DeviceIdType.MESH
CHUNK = 16
WINDOW = 2
PARTS = 2


def kernel(n, occupied, virtual, amp, integrals, pair, column, out, dress, recv,
           held, tile, total, send_sem, recv_sem, load_sem, held_sem):
    me = lax.axis_index("dev")
    rows = out.shape[1]
    count = integrals.shape[0]
    width = integrals.shape[1]
    chunks = rows // CHUNK
    blocks = count // virtual
    window = min(WINDOW, chunks)

    load_integrals = pltpu.make_async_copy(integrals, held, held_sem)
    load_integrals.start()

    barrier = pltpu.get_barrier_semaphore()
    for o in range(1, n):
        pl.semaphore_signal(barrier, inc=1, device_id={"dev": lax.rem(me + o, n)}, device_id_type=MESH)
    pl.semaphore_wait(barrier, n - 1)

    def span(q):
        return pl.ds(pl.multiple_of(q * CHUNK, CHUNK), CHUNK)

    def remote(o, q):
        peer = lax.rem(me + o, n)
        return pltpu.make_async_remote_copy(
            src_ref=amp.at[span(q), pl.ds(pl.multiple_of(peer * count, 128), count)],
            dst_ref=recv.at[o - 1, span(q), :],
            send_sem=send_sem.at[o - 1, q],
            recv_sem=recv_sem.at[o - 1, q],
            device_id={"dev": peer},
            device_id_type=MESH,
        )

    def load(o, q):
        if o == 0:
            source = amp.at[span(q), pl.ds(pl.multiple_of(me * count, 128), count)]
        else:
            source = recv.at[o - 1, span(q), :]
        return pltpu.make_async_copy(source, tile.at[lax.rem(me - o + n, n)], load_sem.at[o])

    order = list(range(n - 1, 0, -1))
    for q in range(window):
        for o in order:
            remote(o, q).start()

    dress[...] = jnp.zeros_like(dress)
    load_integrals.wait()

    def dress_one(c, carry):
        both = jnp.dot(pair[...], held[pl.ds(pl.multiple_of(c * virtual, virtual), virtual), :],
                       preferred_element_type=jnp.float32)
        inner = both[:occupied] + both[occupied:]

        def one_row(i, carry):
            dress[i] += column[c, i] * inner
            return carry

        return lax.fori_loop(0, occupied, one_row, carry)

    lax.fori_loop(0, blocks, dress_one, 0)

    def chunk(q, carry):
        for o in order:
            remote(o, q).wait_send()

        @pl.when(q + window < chunks)
        def _():
            for o in order:
                remote(o, q + window).start()

        for o in order:
            remote(o, q).wait_recv()
        for o in range(n):
            load(o, q).start()
        for o in range(n):
            load(o, q).wait()
        total[...] = jnp.zeros_like(total)

        def term(k, carry):
            part = pl.ds(pl.multiple_of(k * virtual, virtual), virtual)
            total[...] += jnp.dot(tile[:, :, part].reshape(n * CHUNK, virtual), held[part, :],
                                  preferred_element_type=jnp.float32)
            return carry

        lax.fori_loop(0, blocks, term, 0)
        out[:, span(q), :] = total[...].reshape(n, CHUNK, width)
        return carry

    lax.fori_loop(0, chunks, chunk, 0)


def combine(n, g, whole, out, half, summed, got, mine, zgot, full,
            half_send, half_recv, got_send, got_recv, z_send, z_recv, full_send, full_recv):
    me = lax.axis_index("dev")
    z = lax.axis_index("grp")
    m = n // 2
    side = lax.rem(me, 2)
    base = me // 2
    mate = me + 1 - 2 * side
    piece = out.shape[0] // g
    wide = out.shape[1] // PARTS

    def cols(h):
        return pl.ds(h * wide, wide)

    def peer(o):
        return 2 * lax.rem(base + o, m) + side

    def zpeer(o):
        return lax.rem(z + o, g)

    barrier = pltpu.get_barrier_semaphore()
    for target in [mate] + [peer(o) for o in range(1, m)]:
        pl.semaphore_signal(barrier, inc=1, device_id={"dev": target}, device_id_type=MESH)
    for o in range(1, g):
        pl.semaphore_signal(barrier, inc=1, device_id={"grp": zpeer(o)}, device_id_type=MESH)
    pl.semaphore_wait(barrier, 1 + (m - 1) + (g - 1))

    def slab(i):
        return pl.ds(pl.multiple_of(i * piece, piece), piece)

    def to_mate(o, h):
        return pltpu.make_async_remote_copy(
            src_ref=whole.at[lax.rem(base + o, m), 1 - side, :, cols(h)], dst_ref=half.at[o, :, cols(h)],
            send_sem=half_send.at[o, h], recv_sem=half_recv.at[o, h],
            device_id={"dev": mate}, device_id_type=MESH)

    def to_peer(o, h):
        return pltpu.make_async_remote_copy(
            src_ref=summed.at[o, :, cols(h)], dst_ref=got.at[o - 1, :, cols(h)],
            send_sem=got_send.at[o - 1, h], recv_sem=got_recv.at[o - 1, h],
            device_id={"dev": peer(o)}, device_id_type=MESH)

    def to_owner(o, h):
        return pltpu.make_async_remote_copy(
            src_ref=mine.at[slab(zpeer(o)), cols(h)], dst_ref=zgot.at[o - 1, :, cols(h)],
            send_sem=z_send.at[o - 1, h], recv_sem=z_recv.at[o - 1, h],
            device_id={"grp": zpeer(o)}, device_id_type=MESH)

    def to_all(o, slot, h):
        return pltpu.make_async_remote_copy(
            src_ref=full.at[slab(slot), cols(h)], dst_ref=full.at[slab(slot), cols(h)],
            send_sem=full_send.at[o - 1, h], recv_sem=full_recv.at[o - 1, h],
            device_id={"grp": zpeer(o)}, device_id_type=MESH)

    order = list(range(1, m)) + [0]
    for h in range(PARTS):
        for o in order:
            to_mate(o, h).start()
    for h in range(PARTS):
        for o in order:
            to_mate(o, h).wait_recv()
            summed[o, :, cols(h)] = whole[lax.rem(base + o, m), side, :, cols(h)] + half[o, :, cols(h)]
            if o:
                to_peer(o, h).start()
    for h in range(PARTS):
        value = summed[0, :, cols(h)]
        for o in range(1, m):
            to_peer(o, h).wait_recv()
            value = value + got[o - 1, :, cols(h)]
        mine[:, cols(h)] = value
        for o in range(1, g):
            to_owner(o, h).start()
    for h in range(PARTS):
        part = mine[slab(z), cols(h)]
        for o in range(1, g):
            to_owner(o, h).wait_recv()
            part = part + zgot[o - 1, :, cols(h)]
        full[slab(z), cols(h)] = part
        for o in range(1, g):
            to_all(o, z, h).start()
    for h in range(PARTS):
        for o in range(1, g):
            to_all(o, lax.rem(z - o + g, g), h).wait_recv()
        for o in order:
            to_mate(o, h).wait_send()
        for o in range(1, m):
            to_peer(o, h).wait_send()
        for o in range(1, g):
            to_owner(o, h).wait_send()
            to_all(o, z, h).wait_send()
    out[...] = full[...]


def reduce_devices(whole):
    n, g = lax.axis_size("dev"), lax.axis_size("grp")
    share, width = whole.shape[0] // n, whole.shape[1]
    if n % 2 or n < 4 or g < 2 or share % (8 * g) or width % (128 * PARTS):
        whole = whole.reshape(n, share, width)
        mine = lax.all_to_all(whole, "dev", split_axis=0, concat_axis=0, tiled=True).sum(0)
        return lax.all_gather(mine, "grp").sum(0)
    m = n // 2
    vmem = pl.BlockSpec(memory_space=pltpu.VMEM)
    f32 = jnp.float32
    dma = pltpu.SemaphoreType.DMA
    return pl.pallas_call(
        functools.partial(combine, n, g),
        out_shape=jax.ShapeDtypeStruct((share, width), f32),
        in_specs=[vmem],
        out_specs=vmem,
        scratch_shapes=[
            pltpu.VMEM((m, share, width), f32),
            pltpu.VMEM((m, share, width), f32),
            pltpu.VMEM((m - 1, share, width), f32),
            pltpu.VMEM((share, width), f32),
            pltpu.VMEM((g - 1, share // g, width), f32),
            pltpu.VMEM((share, width), f32),
            dma((m, PARTS)), dma((m, PARTS)), dma((m - 1, PARTS)), dma((m - 1, PARTS)),
            dma((g - 1, PARTS)), dma((g - 1, PARTS)), dma((g - 1, PARTS)), dma((g - 1, PARTS)),
        ],
        compiler_params=pltpu.CompilerParams(
            collective_id=1, has_side_effects=True, vmem_limit_bytes=32 * 1024 * 1024
        ),
    )(whole.reshape(m, 2, share, width))


def split_pair(singles):
    high = lax.reduce_precision(singles, 8, 7)
    low = lax.reduce_precision(singles - high, 8, 7)
    return jnp.concatenate([high, low], 0).astype(jnp.bfloat16)


def body(amplitudes, singles, pair_source, integrals):
    n = lax.axis_size("dev")
    occupied, virtual = singles.shape
    rows = amplitudes.shape[0]
    count, width = integrals.shape
    chunks = rows // CHUNK
    blocks = count // virtual
    first = (lax.axis_index("grp") * n + lax.axis_index("dev")) * blocks
    column = lax.dynamic_slice_in_dim(singles.T, first, blocks, 0)
    any_spec = pl.BlockSpec(memory_space=pl.ANY)
    vmem = pl.BlockSpec(memory_space=pltpu.VMEM)
    smem = pl.BlockSpec(memory_space=pltpu.SMEM)
    partial, dress, _ = pl.pallas_call(
        functools.partial(kernel, n, occupied, virtual),
        out_shape=(
            jax.ShapeDtypeStruct((n, rows, width), jnp.float32),
            jax.ShapeDtypeStruct((occupied, occupied, width), jnp.float32),
            jax.ShapeDtypeStruct((n - 1, rows, count), jnp.bfloat16),
        ),
        in_specs=[any_spec, any_spec, vmem, smem],
        out_specs=(vmem, vmem, any_spec),
        scratch_shapes=[
            pltpu.VMEM((count, width), jnp.bfloat16),
            pltpu.VMEM((n, CHUNK, count), jnp.bfloat16),
            pltpu.VMEM((n * CHUNK, width), jnp.float32),
            pltpu.SemaphoreType.DMA((n - 1, chunks)),
            pltpu.SemaphoreType.DMA((n - 1, chunks)),
            pltpu.SemaphoreType.DMA((n,)),
            pltpu.SemaphoreType.DMA,
        ],
        compiler_params=pltpu.CompilerParams(
            collective_id=0, has_side_effects=True, vmem_limit_bytes=48 * 1024 * 1024
        ),
        cost_estimate=pl.CostEstimate(
            flops=2 * n * rows * count * width,
            bytes_accessed=4 * n * rows * count + 2 * count * width,
            transcendentals=0,
        ),
    )(amplitudes, integrals, split_pair(singles), column)
    whole = jnp.take(partial.reshape(n * rows, width), pair_source, axis=0)
    whole = whole + dress.reshape(n * rows, width)
    return reduce_devices(whole)


def solution(mesh):
    placed = (P("dev", "grp"), P(), P(), P(("grp", "dev"), None))
    return jax.shard_map(
        body, mesh=mesh, in_specs=placed, out_specs=P("dev", None), check_vma=False
    )
```
